32 devices in a mesh: group: 1, expert: 32 (over z, y, x, core).
Axes of the slice: x: 2, y: 2, z: 4, core: 2. Of those that a mesh axis runs over, the one named last changes fastest.
Arguments:
- tokens: bfloat16 [256, 2880], P(('group', 'expert')), may hold values from -6 to 6
- routes: int32 [256, 4], P(('group', 'expert')), may hold values from 0 to 7, all different within a row; in each aligned block of 8 rows (0 to 7, 8 to 15, ...) at most 8 rows name the same one
- gates: bfloat16 [256, 4], P(('group', 'expert')), may hold values from 0.099609375 to 1
- w_gate: bfloat16 [32, 2880, 360], P('expert'), may hold values from -0.109375 to 0.109375
- w_up: bfloat16 [32, 2880, 360], P('expert'), may hold values from -0.109375 to 0.109375
- w_down: bfloat16 [32, 360, 2880], P('expert'), may hold values from -0.15625 to 0.15625
- w_enc: bfloat16 [2880, 16384], P(None, 'expert'), may hold values from -0.109375 to 0.109375
- b_enc: float32 [16384], P('expert'), may hold values from -1 to 0.25
- w_dec: bfloat16 [16384, 2880], P('expert'), may hold values from -0.046875 to 0.046875
- b_dec: float32 [2880], replicated, may hold values from -3 to 3
Outputs:
- residual: bfloat16 [256, 2880], P(('group', 'expert'))
The draws below stay inside these ranges and needn't reach their ends.
Inputs may be any that keep to these rules, and one draw needn't show every extreme that they name: `routes`: each row names 4 different experts. Among the rows of one device no expert is named by more than 8 rows, a bound that some block reaches.
All inputs are finite; a program needn't handle non-finite values.
Results may differ from the reference program's by a relative error of at most 0.0048.
Values may be sent and summed in bfloat16 or wider, within the bound.
A program may use at most 128 MiB of HBM per device.

```python
import math
import jax
import jax.numpy as jnp
import numpy as np
from jax import lax

D = 2880
FF = 1440
SLABS = 4
TOPK = 4
TOK_DEV = 8
FF_SLAB = 360
EXPERTS = 8
TOKENS = 256
FEATURES = 16384
CAP = 8


def block_scale(stream_key, dims, split, smallest, largest):
    factor_of, own = 1.0, jax.random.fold_in(stream_key, 6)
    for axis_at, parts in split:
        draws = jnp.exp(jax.random.uniform(jax.random.fold_in(own, axis_at), (parts,), jnp.float32, smallest / len(split), largest / len(split)))
        factor_of = factor_of * jnp.repeat(draws, dims[axis_at] // parts).reshape([-1 if axis == axis_at else 1 for axis in range(len(dims))])
    return factor_of


def deal_out(rng, own, number, rows, count, top, reach, lean):
    order = jax.random.permutation(rng, count)
    crowded, usual = load_shares(count, rows * top, reach, lean, True), load_shares(count, rows * top, reach, lean, False)
    places = jnp.arange(count)

    def named(lengths, offset_by):
        used = int((lengths > 0).sum())
        fixed = max(1, used // 4)
        shifted = fixed + (places - fixed + offset_by * (used - fixed)) % max(1, count - fixed)
        return jnp.zeros((count,), jnp.int32).at[order[jnp.where(places < fixed, places, shifted)]].set(jnp.asarray(lengths, jnp.int32))

    lengths = jnp.where(number % 4 == 0, named(crowded, number // 4), named(usual, number - number // 4 - 1))
    mixed = jax.random.permutation(jax.random.fold_in(own, 3), count)
    giver, taker = mixed[0:count // 2 * 2:2], mixed[1:count // 2 * 2:2]
    room = jnp.minimum(lengths[giver] - 1, reach - lengths[taker]) // 2
    room = jnp.where((giver == order[0]) | (taker == order[0]) | (lengths[taker] == 0), 0, jnp.maximum(room, 0))
    shifted = jax.random.randint(jax.random.fold_in(own, 4), (count // 2,), 0, 1 << 20) % (room + 1)
    lengths = lengths.at[giver].add(-shifted).at[taker].add(shifted)
    labels = jnp.searchsorted(jnp.cumsum(lengths), jnp.arange(rows * top), side="right").astype(jnp.int32)
    listing = labels.reshape(top, rows).T
    listing = listing[jax.random.permutation(jax.random.fold_in(own, 1), rows)]
    offset_by = jax.random.randint(jax.random.fold_in(own, 2), (rows, 1), 0, top)
    return jnp.take_along_axis(listing, (jnp.arange(top)[None, :] + offset_by) % top, axis=1)


def load_shares(amount, total, most, skew, full):
    weights = [(1 << 20) // math.isqrt(grade ** skew) + 1 for grade in range(1, amount + 1)]
    largest = most if full else min(most, max(-(-total // amount), total * weights[0] // sum(weights)))
    least = 1 if total - largest >= amount - 1 else 0
    holding, rest = [largest] + [least] * (amount - 1), total - largest - least * (amount - 1)
    while rest > 0:
        candidates = [i for i in range(1, amount) if holding[i] < largest] or [i for i in range(1, amount) if holding[i] < most]
        whole, left = sum([weights[i] for i in candidates]), rest
        for i in candidates:
            more = min(most - holding[i], max(1, left * weights[i] // whole), rest)
            holding[i] = holding[i] + more
            rest = rest - more
    return np.array(holding)


def normal_values(stream_key, shape, deviation, limit, split=(), kind=jnp.bfloat16):
    values = deviation * jax.random.normal(stream_key, shape, jnp.float32)
    if split:
        values = values * block_scale(stream_key, shape, split, -0.22, 0.18)
    return jnp.clip(values, -limit, limit).astype(kind)


def setup_inputs(seed: int = 0, part: int = 0) -> dict:
    keys = jax.random.split(jax.random.key(seed), 11)
    part_keys = jax.random.split(jax.random.fold_in(keys[10], part), 11)
    tokens = normal_values(part_keys[0], (TOKENS, D), 1.0, 6.0, ((0, 32),))
    routes_keys = jax.random.split(jax.random.fold_in(part_keys[1], 1), TOKENS // TOK_DEV)
    routes_turns = jax.random.permutation(jax.random.fold_in(part_keys[1], 3), TOKENS // TOK_DEV)
    routes = jax.vmap(lambda own, number: deal_out(jax.random.fold_in(part_keys[1], 2), own, number, TOK_DEV, EXPERTS, TOPK, CAP, 2))(routes_keys, routes_turns).reshape((TOKENS, TOPK))
    gates = jnp.clip(0.099609375 + 0.9003906 * jax.random.uniform(part_keys[2], (TOKENS, TOPK), jnp.float32) ** block_scale(part_keys[2], (TOKENS, TOPK), ((0, 32),), -0.2, 0.2), 0.099609375, 1.0).astype(jnp.bfloat16)
    w_gate = normal_values(keys[3], (EXPERTS * SLABS, D, FF_SLAB), D ** -0.5, 0.109375, ((0, 32),))
    w_up = normal_values(keys[4], (EXPERTS * SLABS, D, FF_SLAB), D ** -0.5, 0.109375, ((0, 32),))
    w_down = normal_values(keys[5], (EXPERTS * SLABS, FF_SLAB, D), FF ** -0.5, 0.15625, ((0, 32),))
    w_enc = normal_values(keys[6], (D, FEATURES), D ** -0.5, 0.109375, ((1, 32),))
    b_enc = jnp.clip(-1.0 + 1.25 * jax.random.uniform(keys[7], (FEATURES,), jnp.float32) ** block_scale(keys[7], (FEATURES,), ((0, 32),), -0.2, 0.2), -1.0, 0.25)
    w_dec = normal_values(keys[8], (FEATURES, D), FEATURES ** -0.5, 0.046875, ((0, 32),))
    b_dec = normal_values(keys[9], (D,), 0.5, 3.0, (), jnp.float32)
    return dict(tokens=tokens, routes=routes, gates=gates, w_gate=w_gate, w_up=w_up, w_down=w_down, w_enc=w_enc, b_enc=b_enc, w_dec=w_dec, b_dec=b_dec)


def reference(tokens, routes, gates, w_gate, w_up, w_down, w_enc, b_enc, w_dec, b_dec):
    gate_full = w_gate.reshape(EXPERTS, SLABS, D, FF_SLAB).transpose(0, 2, 1, 3).reshape(EXPERTS, D, FF)
    up_full = w_up.reshape(EXPERTS, SLABS, D, FF_SLAB).transpose(0, 2, 1, 3).reshape(EXPERTS, D, FF)
    down_full = w_down.reshape(EXPERTS, FF, D)
    chosen = routes[:, :, None] == jnp.arange(EXPERTS, dtype=jnp.int32)[None, None, :]
    weights = jnp.sum(jnp.where(chosen, gates.astype(jnp.float32)[:, :, None], jnp.float32(0.0)), axis=1)

    def one_expert(total, items):
        gate_w, up_w, down_w, column = items
        gate_pre = jnp.dot(tokens, gate_w, preferred_element_type=jnp.float32)
        up_pre = jnp.dot(tokens, up_w, preferred_element_type=jnp.float32)
        hidden = ((up_pre + 1.0) * gate_pre * jax.nn.sigmoid(1.702 * gate_pre)).astype(jnp.bfloat16)
        output = jnp.dot(hidden, down_w, preferred_element_type=jnp.float32)
        return total + column[:, None] * output, None

    start = jnp.zeros((TOKENS, D), jnp.float32)
    layer_out = lax.scan(one_expert, start, (gate_full, up_full, down_full, weights.T))[0]
    features = jnp.maximum(jnp.dot(tokens, w_enc, preferred_element_type=jnp.float32) + b_enc, 0.0).astype(jnp.bfloat16)
    prediction = jnp.dot(features, w_dec, preferred_element_type=jnp.float32) + b_dec
    return (layer_out - prediction).astype(jnp.bfloat16)
```

```python
import functools

import jax
import jax.numpy as jnp
from jax import lax
from jax.experimental import pallas as pl
from jax.experimental.pallas import tpu as pltpu
from jax.sharding import PartitionSpec as P

SLABS = 4
LANES = 128
F32 = jnp.float32
BF16 = jnp.bfloat16


def cut(width, parts):
    tiles = -(-width // LANES)
    edges = [LANES * (tiles * i // parts) for i in range(parts)] + [width]
    return list(zip(edges[:-1], edges[1:]))


class Plan:
    def __init__(self, n, d):
        self.n, self.d = n, d
        self.bits = n.bit_length() - 1
        self.half = n // 2
        self.rows = 8 * n
        self.wide = -(-(d + n // SLABS) // LANES) * LANES
        tiles = self.wide // LANES
        self.left = LANES * (tiles // 2)
        self.right = self.wide - self.left
        self.chunks = cut(d, 2)
        low = list(range(self.bits - 2, 0, -1))
        swapped = low[:-2] + low[-2:][::-1]
        self.orders = [low + [0], swapped + [0]]

    def weight(self, j):
        return 2 ** (self.bits - 2 - j)

    def split(self, done):
        run, rest = 1, list(done)
        j = self.bits - 2
        while j in rest:
            rest.remove(j)
            run *= 2
            j -= 1
        offsets = [0]
        for j in rest:
            offsets = offsets + [o + self.weight(j) for o in offsets]
        return run, rest, sorted(offsets)


def body(plan, tokens, routes, gates, w_gate, w_up, w_down, w_enc, b_enc, w_dec, b_dec, out, *scratch):
    p = plan
    chunks = len(p.chunks)
    (v_gate, v_up, v_down, v_enc, v_dec, flat, fold, fold_in, x_left, x_right, hid, feat) = scratch[:12]
    rest = list(scratch[12:])
    acc = [rest.pop(0) for _ in range(chunks)]
    send = [[rest.pop(0) for _ in range(p.bits - 1)] for _ in range(chunks)]
    recv = [[rest.pop(0) for _ in range(p.bits - 1)] for _ in range(chunks)]
    last = [rest.pop(0) for _ in range(chunks)]
    load_sem, ag_send, ag_recv, rs_send, rs_recv = rest

    me = lax.axis_index("expert")
    bit = [(me // 2**j) % 2 for j in range(p.bits)]
    partner = [me + (1 - 2 * bit[j]) * 2**j for j in range(p.bits)]
    top = p.bits - 1

    loads = [
        pltpu.make_async_copy(src, dst, load_sem.at[i])
        for i, (src, dst) in enumerate(
            [
                (w_gate.at[0], v_gate),
                (w_up.at[0], v_up),
                (w_enc, v_enc),
                (w_down.at[0], v_down),
                (w_dec, v_dec),
            ]
        )
    ]
    for load in loads:
        load.start()

    barrier = pltpu.get_barrier_semaphore()
    for j in range(p.bits):
        pl.semaphore_signal(
            barrier, inc=1, device_id={"expert": partner[j]}, device_id_type=pl.DeviceIdType.MESH
        )

    start = p.d // LANES * LANES
    lane = lax.broadcasted_iota(jnp.int32, (8, p.wide - start), 1) - (p.d - start)
    dense = jnp.zeros((8, p.wide - start), F32)
    chosen = routes[...]
    weights = gates[...].astype(F32)
    for k in range(routes.shape[1]):
        dense = dense + jnp.where(lane == chosen[:, k : k + 1], weights[:, k : k + 1], 0.0)
    flat[:, start:] = dense
    flat[:, : p.d] = tokens[...].astype(F32)
    mine = flat[...]
    lead = mine[:, : p.left]
    if p.right > p.left:
        lead = jnp.concatenate([lead, jnp.zeros((8, p.right - p.left), F32)], axis=1)
    fold[...] = jnp.concatenate([lead, mine[:, p.left :]], axis=0).astype(BF16)

    pl.semaphore_wait(barrier, p.bits)

    count = [0]

    def copy(src, dst, to, sems):
        i = count[0]
        count[0] += 1
        return pltpu.make_async_remote_copy(
            src_ref=src,
            dst_ref=dst,
            send_sem=sems[0].at[i],
            recv_sem=sems[1].at[i],
            device_id={"expert": to},
            device_id_type=pl.DeviceIdType.MESH,
        )

    sent = []
    first = copy(fold, fold_in, partner[top], (ag_send, ag_recv))
    first.start()
    sent.append(first)

    def base(fixed):
        total = 0
        for j in fixed:
            total = total + bit[j] * p.weight(j)
        return total

    low_bits = list(range(p.bits - 1))
    block = pl.multiple_of(base(low_bits) * 16, 16)
    first.wait_recv()
    other = fold_in[...].astype(F32)
    for half, x in ((0, x_left), (1, x_right)):
        width = x.shape[1]
        a = mine[:, : p.left] if half == 0 else mine[:, p.left :]
        b = other[8 * half : 8 * half + 8, :width]
        low = jnp.where(bit[top] == 0, a, b)
        high = jnp.where(bit[top] == 0, b, a)
        x[pl.ds(block, 16), :] = jnp.concatenate([low, high], axis=0).astype(BF16)

    pending = [[], []]
    for s in range(p.bits - 1):
        for half, x in ((0, x_left), (1, x_right)):
            for c in pending[half]:
                c.wait_recv()
            done = p.orders[half][:s]
            j = p.orders[half][s]
            run, extra, offsets = p.split(done)
            fixed = [b for b in low_bits if b not in done]
            origin = base(fixed)
            pending[half] = []
            for o in offsets:
                rows = pl.ds(pl.multiple_of((origin + o) * 16, 16), 16 * run)
                c = copy(x.at[rows], x.at[rows], partner[j], (ag_send, ag_recv))
                c.start()
                sent.append(c)
                pending[half].append(c)
    for half in (0, 1):
        for c in pending[half]:
            c.wait_recv()

    def project(w, cols=None):
        left, right = x_left[...], x_right[:, : p.d - p.left]
        return jnp.dot(left, w[: p.left, :], preferred_element_type=F32) + jnp.dot(
            right, w[p.left :, :], preferred_element_type=F32
        )

    loads[0].wait()
    gate_pre = project(v_gate)
    loads[1].wait()
    up_pre = project(v_up)
    hid[...] = ((up_pre + 1.0) * gate_pre * jax.nn.sigmoid(1.702 * gate_pre)).astype(BF16)
    loads[2].wait()
    feat[...] = jnp.maximum(project(v_enc) + b_enc[...], 0.0).astype(BF16)

    tail = x_right[:, start - p.left :].astype(F32)
    lane = lax.broadcasted_iota(jnp.int32, tail.shape, 1) - (p.d - start)
    scale = jnp.sum(jnp.where(lane == me // SLABS, tail, 0.0), axis=1, keepdims=True)

    count[0] = 0
    flights = [None] * chunks

    def pieces(c, s, own):
        order = p.orders[c % 2][::-1]
        j = order[s]
        fixed = order[: s + 1]
        run, extra, offsets = p.split([b for b in low_bits if b not in fixed])
        origin = base(order[:s]) + (bit[j] if own else 1 - bit[j]) * p.weight(j)
        return [pl.ds(pl.multiple_of((origin + o) * 16, 16), 16 * run) for o in offsets]

    def send_stage(c, s):
        if s < p.bits - 1:
            at = 0
            for rows in pieces(c, s, False):
                send[c][s][at : at + rows.size, :] = acc[c][rows, :].astype(BF16)
                at += rows.size
            to = partner[p.orders[c % 2][::-1][s]]
            flights[c] = copy(send[c][s], recv[c][s], to, (rs_send, rs_recv))
        else:
            rows = pl.ds(pl.multiple_of(block + 8 * (1 - bit[top]), 8), 8)
            flights[c] = copy(acc[c].at[rows], last[c], partner[top], (rs_send, rs_recv))
        flights[c].start()
        sent.append(flights[c])

    loads[3].wait()
    loads[4].wait()
    for c, (lo, hi) in enumerate(p.chunks):
        acc[c][...] = scale * jnp.dot(
            hid[...], v_down[:, lo:hi], preferred_element_type=F32
        ) - jnp.dot(feat[...], v_dec[:, lo:hi], preferred_element_type=F32)
        send_stage(c, 0)
    for s in range(p.bits - 1):
        for c in range(chunks):
            flights[c].wait_recv()
            at = 0
            for rows in pieces(c, s, True):
                acc[c][rows, :] = acc[c][rows, :] + recv[c][s][at : at + rows.size, :].astype(F32)
                at += rows.size
            send_stage(c, s + 1)
    rows = pl.ds(pl.multiple_of(block + 8 * bit[top], 8), 8)
    for c, (lo, hi) in enumerate(p.chunks):
        flights[c].wait_recv()
        out[:, lo:hi] = (acc[c][rows, :] + last[c][...] - b_dec[:, lo:hi]).astype(BF16)
    for c in sent:
        c.wait_send()


def shards(tokens, routes, gates, w_gate, w_up, w_down, w_enc, b_enc, w_dec, b_dec):
    n = lax.axis_size("expert")
    d = tokens.shape[1]
    p = Plan(n, d)
    widths = [hi - lo for lo, hi in p.chunks]
    stage_rows = [p.rows // 2 ** (s + 1) for s in range(p.bits - 1)]
    ag = 1 + sum(len(p.split(o[:s])[2]) for o in p.orders for s in range(p.bits - 1))
    rs = len(widths) * p.bits
    vmem = pl.BlockSpec(memory_space=pltpu.VMEM)
    hbm = pl.BlockSpec(memory_space=pl.ANY)
    scratch = [
        pltpu.VMEM(w_gate.shape[1:], BF16),
        pltpu.VMEM(w_up.shape[1:], BF16),
        pltpu.VMEM(w_down.shape[1:], BF16),
        pltpu.VMEM(w_enc.shape, BF16),
        pltpu.VMEM(w_dec.shape, BF16),
        pltpu.VMEM((8, p.wide), F32),
        pltpu.VMEM((16, p.right), BF16),
        pltpu.VMEM((16, p.right), BF16),
        pltpu.VMEM((p.rows, p.left), BF16),
        pltpu.VMEM((p.rows, p.right), BF16),
        pltpu.VMEM((p.rows, w_gate.shape[2]), BF16),
        pltpu.VMEM((p.rows, w_enc.shape[1]), BF16),
    ]
    scratch += [pltpu.VMEM((p.rows, w), F32) for w in widths]
    scratch += [pltpu.VMEM((r, w), BF16) for w in widths for r in stage_rows] * 2
    scratch += [pltpu.VMEM((8, w), F32) for w in widths]
    scratch += [pltpu.SemaphoreType.DMA((k,)) for k in (5, ag, ag, rs, rs)]
    flops = 2 * p.rows * d * (3 * w_gate.shape[2] + 2 * w_enc.shape[1])
    size = 2 * d * (3 * w_gate.shape[2] + 2 * w_enc.shape[1])
    return pl.pallas_call(
        functools.partial(body, p),
        out_shape=jax.ShapeDtypeStruct(tokens.shape, BF16),
        in_specs=[vmem, vmem, vmem, hbm, hbm, hbm, hbm, vmem, hbm, vmem],
        out_specs=vmem,
        scratch_shapes=scratch,
        cost_estimate=pl.CostEstimate(flops=flops, bytes_accessed=size, transcendentals=0),
        compiler_params=pltpu.CompilerParams(
            collective_id=0, has_side_effects=True, vmem_limit_bytes=56 * 2**20
        ),
    )(
        tokens,
        routes,
        gates,
        w_gate,
        w_up,
        w_down,
        w_enc,
        b_enc.reshape(1, -1),
        w_dec,
        b_dec.reshape(1, -1),
    )


def solution(mesh):
    in_specs = (
        P(("group", "expert"), None),
        P(("group", "expert"), None),
        P(("group", "expert"), None),
        P("expert", None, None),
        P("expert", None, None),
        P("expert", None, None),
        P(None, "expert"),
        P("expert"),
        P("expert", None),
        P(),
    )
    out_specs = P(("group", "expert"), None)
    return jax.shard_map(shards, mesh=mesh, in_specs=in_specs, out_specs=out_specs, check_vma=False)
```

```python
import functools

import jax
import jax.numpy as jnp
from jax import lax
from jax.experimental import pallas as pl
from jax.experimental.pallas import tpu as pltpu
from jax.sharding import PartitionSpec as P

SLABS = 4
LANES = 128
F32 = jnp.float32
BF16 = jnp.bfloat16


def cut(width, parts):
    tiles = -(-width // LANES)
    edges = [LANES * (tiles * i // parts) for i in range(parts)] + [width]
    return list(zip(edges[:-1], edges[1:]))


class Plan:
    def __init__(self, n, d):
        self.n, self.d = n, d
        self.bits = n.bit_length() - 1
        self.half = n // 2
        self.rows = 8 * n
        self.wide = -(-(d + n // SLABS) // LANES) * LANES
        tiles = self.wide // LANES
        self.left = LANES * (tiles // 2)
        self.right = self.wide - self.left
        self.chunks = cut(d, 2)
        low = list(range(self.bits - 2, 0, -1))
        swapped = low[:-2] + low[-2:][::-1]
        self.orders = [low + [0], swapped + [0]]

    def weight(self, j):
        return 2 ** (self.bits - 2 - j)

    def split(self, done):
        run, rest = 1, list(done)
        j = self.bits - 2
        while j in rest:
            rest.remove(j)
            run *= 2
            j -= 1
        offsets = [0]
        for j in rest:
            offsets = offsets + [o + self.weight(j) for o in offsets]
        return run, rest, sorted(offsets)


def body(plan, tokens, routes, gates, w_gate, w_up, w_down, w_enc, b_enc, w_dec, out, *scratch):
    p = plan
    chunks = len(p.chunks)
    (v_gate, v_up, v_down, v_enc, v_dec, flat, fold, fold_in, x_left, x_right, hid, feat) = scratch[:12]
    rest = list(scratch[12:])
    acc = [rest.pop(0) for _ in range(chunks)]
    send = [[rest.pop(0) for _ in range(p.bits - 1)] for _ in range(chunks)]
    recv = [[rest.pop(0) for _ in range(p.bits - 1)] for _ in range(chunks)]
    last = [rest.pop(0) for _ in range(chunks)]
    load_sem, ag_send, ag_recv, rs_send, rs_recv = rest

    me = lax.axis_index("expert")
    bit = [(me // 2**j) % 2 for j in range(p.bits)]
    partner = [me + (1 - 2 * bit[j]) * 2**j for j in range(p.bits)]
    top = p.bits - 1

    loads = [
        pltpu.make_async_copy(src, dst, load_sem.at[i])
        for i, (src, dst) in enumerate(
            [
                (w_gate.at[0], v_gate),
                (w_up.at[0], v_up),
                (w_enc, v_enc),
                (w_down.at[0], v_down),
                (w_dec, v_dec),
            ]
        )
    ]
    for load in loads:
        load.start()

    barrier = pltpu.get_barrier_semaphore()
    for j in range(p.bits):
        pl.semaphore_signal(
            barrier, inc=1, device_id={"expert": partner[j]}, device_id_type=pl.DeviceIdType.MESH
        )

    start = p.d // LANES * LANES
    lane = lax.broadcasted_iota(jnp.int32, (8, p.wide - start), 1) - (p.d - start)
    dense = jnp.zeros((8, p.wide - start), F32)
    eye = lax.broadcasted_iota(jnp.int32, (8, 8), 0) == lax.broadcasted_iota(jnp.int32, (8, 8), 1)

    def column(row):
        return jnp.sum(jnp.where(eye, row, 0.0), axis=1, keepdims=True)

    chosen = routes[...].astype(F32)
    weights = gates[...].astype(F32)
    for k in range(routes.shape[0]):
        dense = dense + jnp.where(
            lane.astype(F32) == column(chosen[k : k + 1, :]), column(weights[k : k + 1, :]), 0.0
        )
    flat[:, start:] = dense
    flat[:, : p.d] = tokens[...].astype(F32)
    mine = flat[...]
    lead = mine[:, : p.left]
    if p.right > p.left:
        lead = jnp.concatenate([lead, jnp.zeros((8, p.right - p.left), F32)], axis=1)
    fold[...] = jnp.concatenate([lead, mine[:, p.left :]], axis=0).astype(BF16)

    pl.semaphore_wait(barrier, p.bits)

    count = [0]

    def copy(src, dst, to, sems):
        i = count[0]
        count[0] += 1
        return pltpu.make_async_remote_copy(
            src_ref=src,
            dst_ref=dst,
            send_sem=sems[0].at[i],
            recv_sem=sems[1].at[i],
            device_id={"expert": to},
            device_id_type=pl.DeviceIdType.MESH,
        )

    sent = []
    first = copy(fold, fold_in, partner[top], (ag_send, ag_recv))
    first.start()
    sent.append(first)

    def base(fixed):
        total = 0
        for j in fixed:
            total = total + bit[j] * p.weight(j)
        return total

    low_bits = list(range(p.bits - 1))
    block = pl.multiple_of(base(low_bits) * 16, 16)
    first.wait_recv()
    other = fold_in[...].astype(F32)
    for half, x in ((0, x_left), (1, x_right)):
        width = x.shape[1]
        a = mine[:, : p.left] if half == 0 else mine[:, p.left :]
        b = other[8 * half : 8 * half + 8, :width]
        low = jnp.where(bit[top] == 0, a, b)
        high = jnp.where(bit[top] == 0, b, a)
        x[pl.ds(block, 16), :] = jnp.concatenate([low, high], axis=0).astype(BF16)

    pending = [[], []]
    for s in range(p.bits - 1):
        for half, x in ((0, x_left), (1, x_right)):
            for c in pending[half]:
                c.wait_recv()
            done = p.orders[half][:s]
            j = p.orders[half][s]
            run, extra, offsets = p.split(done)
            fixed = [b for b in low_bits if b not in done]
            origin = base(fixed)
            pending[half] = []
            for o in offsets:
                rows = pl.ds(pl.multiple_of((origin + o) * 16, 16), 16 * run)
                c = copy(x.at[rows], x.at[rows], partner[j], (ag_send, ag_recv))
                c.start()
                sent.append(c)
                pending[half].append(c)
    for half in (0, 1):
        for c in pending[half]:
            c.wait_recv()

    def by_rows(a, b):
        return lax.dot_general(a, b, (((1,), (1,)), ((), ())), preferred_element_type=F32)

    def project_rows(w):
        left, right = x_left[...], x_right[:, : p.d - p.left]
        return by_rows(left, w[:, : p.left]) + by_rows(right, w[:, p.left :])

    def project(w):
        left, right = x_left[...], x_right[:, : p.d - p.left]
        return jnp.dot(left, w[: p.left, :], preferred_element_type=F32) + jnp.dot(
            right, w[p.left :, :], preferred_element_type=F32
        )

    loads[0].wait()
    gate_pre = project_rows(v_gate)
    loads[1].wait()
    up_pre = project_rows(v_up)
    hid[...] = ((up_pre + 1.0) * gate_pre * jax.nn.sigmoid(1.702 * gate_pre)).astype(BF16)
    loads[2].wait()
    feat[...] = jnp.maximum(project(v_enc) + b_enc[...], 0.0).astype(BF16)

    tail = x_right[:, start - p.left :].astype(F32)
    lane = lax.broadcasted_iota(jnp.int32, tail.shape, 1) - (p.d - start)
    scale = jnp.sum(jnp.where(lane == me // SLABS, tail, 0.0), axis=1, keepdims=True)

    count[0] = 0
    flights = [None] * chunks

    def pieces(c, s, own):
        order = p.orders[c % 2][::-1]
        j = order[s]
        fixed = order[: s + 1]
        run, extra, offsets = p.split([b for b in low_bits if b not in fixed])
        origin = base(order[:s]) + (bit[j] if own else 1 - bit[j]) * p.weight(j)
        return [pl.ds(pl.multiple_of((origin + o) * 16, 16), 16 * run) for o in offsets]

    def send_stage(c, s):
        if s < p.bits - 1:
            at = 0
            for rows in pieces(c, s, False):
                send[c][s][at : at + rows.size, :] = acc[c][rows, :].astype(BF16)
                at += rows.size
            to = partner[p.orders[c % 2][::-1][s]]
            flights[c] = copy(send[c][s], recv[c][s], to, (rs_send, rs_recv))
        else:
            rows = pl.ds(pl.multiple_of(block + 8 * (1 - bit[top]), 8), 8)
            flights[c] = copy(acc[c].at[rows], last[c], partner[top], (rs_send, rs_recv))
        flights[c].start()
        sent.append(flights[c])

    loads[3].wait()
    loads[4].wait()
    for c, (lo, hi) in enumerate(p.chunks):
        acc[c][...] = scale * jnp.dot(
            hid[...], v_down[:, lo:hi], preferred_element_type=F32
        ) - by_rows(feat[...], v_dec[lo:hi, :])
        send_stage(c, 0)
    for s in range(p.bits - 1):
        for c in range(chunks):
            flights[c].wait_recv()
            at = 0
            for rows in pieces(c, s, True):
                acc[c][rows, :] = acc[c][rows, :] + recv[c][s][at : at + rows.size, :].astype(F32)
                at += rows.size
            send_stage(c, s + 1)
    rows = pl.ds(pl.multiple_of(block + 8 * bit[top], 8), 8)
    for c, (lo, hi) in enumerate(p.chunks):
        flights[c].wait_recv()
        out[:, lo:hi] = acc[c][rows, :] + last[c][...]
    for c in sent:
        c.wait_send()


def shards(tokens, routes, gates, w_gate, w_up, w_down, w_enc, b_enc, w_dec, b_dec):
    n = lax.axis_size("expert")
    d = tokens.shape[1]
    p = Plan(n, d)
    widths = [hi - lo for lo, hi in p.chunks]
    stage_rows = [p.rows // 2 ** (s + 1) for s in range(p.bits - 1)]
    ag = 1 + sum(len(p.split(o[:s])[2]) for o in p.orders for s in range(p.bits - 1))
    rs = len(widths) * p.bits
    vmem = pl.BlockSpec(memory_space=pltpu.VMEM)
    hbm = pl.BlockSpec(memory_space=pl.ANY)
    scratch = [
        pltpu.VMEM(w_gate.shape[:0:-1], BF16),
        pltpu.VMEM(w_up.shape[:0:-1], BF16),
        pltpu.VMEM(w_down.shape[1:], BF16),
        pltpu.VMEM(w_enc.shape, BF16),
        pltpu.VMEM(w_dec.shape[::-1], BF16),
        pltpu.VMEM((8, p.wide), F32),
        pltpu.VMEM((16, p.right), BF16),
        pltpu.VMEM((16, p.right), BF16),
        pltpu.VMEM((p.rows, p.left), BF16),
        pltpu.VMEM((p.rows, p.right), BF16),
        pltpu.VMEM((p.rows, w_gate.shape[2]), BF16),
        pltpu.VMEM((p.rows, w_enc.shape[1]), BF16),
    ]
    scratch += [pltpu.VMEM((p.rows, w), F32) for w in widths]
    scratch += [pltpu.VMEM((r, w), BF16) for w in widths for r in stage_rows] * 2
    scratch += [pltpu.VMEM((8, w), F32) for w in widths]
    scratch += [pltpu.SemaphoreType.DMA((k,)) for k in (5, ag, ag, rs, rs)]
    flops = 2 * p.rows * d * (3 * w_gate.shape[2] + 2 * w_enc.shape[1])
    size = 2 * d * (3 * w_gate.shape[2] + 2 * w_enc.shape[1])
    total = pl.pallas_call(
        functools.partial(body, p),
        out_shape=jax.ShapeDtypeStruct(tokens.shape, F32),
        in_specs=[vmem, vmem, vmem, hbm, hbm, hbm, hbm, vmem, hbm],
        out_specs=vmem,
        scratch_shapes=scratch,
        cost_estimate=pl.CostEstimate(flops=flops, bytes_accessed=size, transcendentals=0),
        compiler_params=pltpu.CompilerParams(
            collective_id=0, has_side_effects=True, vmem_limit_bytes=56 * 2**20
        ),
    )(
        tokens,
        routes.T,
        gates.T,
        w_gate.transpose(0, 2, 1),
        w_up.transpose(0, 2, 1),
        w_down,
        w_enc,
        b_enc.reshape(1, -1),
        w_dec.T,
    )
    return (total - b_dec).astype(BF16)


def solution(mesh):
    in_specs = (
        P(("group", "expert"), None),
        P(("group", "expert"), None),
        P(("group", "expert"), None),
        P("expert", None, None),
        P("expert", None, None),
        P("expert", None, None),
        P(None, "expert"),
        P("expert"),
        P("expert", None),
        P(),
    )
    out_specs = P(("group", "expert"), None)
    return jax.shard_map(shards, mesh=mesh, in_specs=in_specs, out_specs=out_specs, check_vma=False)
```

```python
import functools

import jax
import jax.numpy as jnp
from jax import lax
from jax.experimental import pallas as pl
from jax.experimental.pallas import tpu as pltpu
from jax.sharding import PartitionSpec as P

SLABS = 4
PAIRS = 2
CHUNKS = 4
LANES = 128
F32 = jnp.float32
BF16 = jnp.bfloat16


def cut(width, parts):
    tiles = -(-width // LANES)
    edges = [LANES * (tiles * i // parts) for i in range(parts)] + [width]
    return list(zip(edges[:-1], edges[1:]))


class Plan:
    def __init__(self, n, d):
        self.n, self.d = n, d
        self.bits = n.bit_length() - 1
        self.half = n // 2
        self.rows = 8 * n
        self.wide = -(-(d + n // SLABS) // LANES) * LANES
        self.parts = cut(self.wide, 2 * PAIRS)
        self.fold = max(hi - lo for lo, hi in self.parts)
        self.chunks = cut(d, CHUNKS)
        low = list(range(self.bits - 2, 0, -1))
        swapped = low[:-2] + low[-2:][::-1]
        self.orders = [low + [0], swapped + [0]]

    def weight(self, j):
        return 2 ** (self.bits - 2 - j)

    def split(self, done):
        run, rest = 1, list(done)
        j = self.bits - 2
        while j in rest:
            rest.remove(j)
            run *= 2
            j -= 1
        offsets = [0]
        for j in rest:
            offsets = offsets + [o + self.weight(j) for o in offsets]
        return run, rest, sorted(offsets)


def body(plan, tokens, routes, gates, w_gate, w_up, w_down, w_enc, b_enc, w_dec, out, *scratch):
    p = plan
    chunks = len(p.chunks)
    (v_gate, v_up, v_down, v_enc, v_dec, flat, fold, fold_in, hid, feat, sum_gate, sum_up, sum_enc) = scratch[:13]
    rest = list(scratch[13:])
    x = [rest.pop(0) for _ in p.parts]
    acc = [rest.pop(0) for _ in range(chunks)]
    send = [[rest.pop(0) for _ in range(p.bits - 1)] for _ in range(chunks)]
    recv = [[rest.pop(0) for _ in range(p.bits - 1)] for _ in range(chunks)]
    last = [rest.pop(0) for _ in range(chunks)]
    load_sem, ag_send, ag_recv, rs_send, rs_recv = rest

    me = lax.axis_index("expert")
    bit = [(me // 2**j) % 2 for j in range(p.bits)]
    partner = [me + (1 - 2 * bit[j]) * 2**j for j in range(p.bits)]
    top = p.bits - 1

    loads = [
        pltpu.make_async_copy(src, dst, load_sem.at[i])
        for i, (src, dst) in enumerate(
            [
                (w_gate.at[0], v_gate),
                (w_up.at[0], v_up),
                (w_enc, v_enc),
                (w_down.at[0], v_down),
                (w_dec, v_dec),
            ]
        )
    ]
    for load in loads:
        load.start()

    barrier = pltpu.get_barrier_semaphore()
    for j in range(p.bits):
        pl.semaphore_signal(
            barrier, inc=1, device_id={"expert": partner[j]}, device_id_type=pl.DeviceIdType.MESH
        )

    start = p.d // LANES * LANES
    lane = lax.broadcasted_iota(jnp.int32, (8, p.wide - start), 1) - (p.d - start)
    dense = jnp.zeros((8, p.wide - start), F32)
    eye = lax.broadcasted_iota(jnp.int32, (8, 8), 0) == lax.broadcasted_iota(jnp.int32, (8, 8), 1)

    def column(row):
        return jnp.sum(jnp.where(eye, row, 0.0), axis=1, keepdims=True)

    chosen = routes[...].astype(F32)
    weights = gates[...].astype(F32)
    for k in range(routes.shape[0]):
        dense = dense + jnp.where(
            lane.astype(F32) == column(chosen[k : k + 1, :]), column(weights[k : k + 1, :]), 0.0
        )
    flat[:, start:] = dense
    flat[:, : p.d] = tokens[...].astype(F32)
    mine = flat[...]

    def part(c):
        lo, hi = p.parts[c]
        return mine[:, lo:hi]

    def padded(value):
        short = p.fold - value.shape[1]
        return jnp.concatenate([value, jnp.zeros((8, short), F32)], axis=1) if short else value

    for q in range(PAIRS):
        both = [padded(part(2 * q)), padded(part(2 * q + 1))]
        fold[q] = jnp.concatenate(both, axis=0).astype(BF16)

    pl.semaphore_wait(barrier, p.bits)

    count = [0]

    def copy(src, dst, to, sems):
        i = count[0]
        count[0] += 1
        return pltpu.make_async_remote_copy(
            src_ref=src,
            dst_ref=dst,
            send_sem=sems[0].at[i],
            recv_sem=sems[1].at[i],
            device_id={"expert": to},
            device_id_type=pl.DeviceIdType.MESH,
        )

    sent = []
    first = [copy(fold.at[q], fold_in.at[q], partner[top], (ag_send, ag_recv)) for q in range(PAIRS)]
    for c in first:
        c.start()
        sent.append(c)

    def base(fixed):
        total = 0
        for j in fixed:
            total = total + bit[j] * p.weight(j)
        return total

    low_bits = list(range(p.bits - 1))
    block = pl.multiple_of(base(low_bits) * 16, 16)
    pending = [[] for _ in p.parts]

    def gather_stage(c, s):
        order = p.orders[c % 2]
        done, j = order[:s], order[s]
        run, extra, offsets = p.split(done)
        origin = base([b for b in low_bits if b not in done])
        pending[c] = []
        for o in offsets:
            rows = pl.ds(pl.multiple_of((origin + o) * 16, 16), 16 * run)
            flight = copy(x[c].at[rows], x[c].at[rows], partner[j], (ag_send, ag_recv))
            flight.start()
            sent.append(flight)
            pending[c].append(flight)

    def arrived(c):
        for flight in pending[c]:
            flight.wait_recv()

    for q in range(PAIRS):
        first[q].wait_recv()
        for half in (0, 1):
            c = 2 * q + half
            a = part(c)
            b = fold_in[q].astype(F32)[8 * half : 8 * half + 8, : a.shape[1]]
            low = jnp.where(bit[top] == 0, a, b)
            high = jnp.where(bit[top] == 0, b, a)
            x[c][pl.ds(block, 16), :] = jnp.concatenate([low, high], axis=0).astype(BF16)
            gather_stage(c, 0)
    for s in range(1, p.bits - 1):
        for c in range(len(p.parts)):
            arrived(c)
            gather_stage(c, s)

    def by_rows(a, b):
        return lax.dot_general(a, b, (((1,), (1,)), ((), ())), preferred_element_type=F32)

    for load in loads[:3]:
        load.wait()
    for c, (lo, hi) in enumerate(p.parts):
        arrived(c)
        hi = min(hi, p.d)
        rows = x[c][:, : hi - lo]
        terms = [
            (sum_gate, by_rows(rows, v_gate[:, lo:hi])),
            (sum_up, by_rows(rows, v_up[:, lo:hi])),
            (sum_enc, jnp.dot(rows, v_enc[lo:hi, :], preferred_element_type=F32)),
        ]
        for total, term in terms:
            total[...] = term if c == 0 else total[...] + term
    gate_pre = sum_gate[...]
    hid[...] = ((sum_up[...] + 1.0) * gate_pre * jax.nn.sigmoid(1.702 * gate_pre)).astype(BF16)
    feat[...] = jnp.maximum(sum_enc[...] + b_enc[...], 0.0).astype(BF16)

    tail = x[-1][:, start - p.parts[-1][0] :].astype(F32)
    lane = lax.broadcasted_iota(jnp.int32, tail.shape, 1) - (p.d - start)
    scale = jnp.sum(jnp.where(lane == me // SLABS, tail, 0.0), axis=1, keepdims=True)

    count[0] = 0
    flights = [None] * chunks

    def pieces(c, s, own):
        order = p.orders[c % 2][::-1]
        j = order[s]
        fixed = order[: s + 1]
        run, extra, offsets = p.split([b for b in low_bits if b not in fixed])
        origin = base(order[:s]) + (bit[j] if own else 1 - bit[j]) * p.weight(j)
        return [pl.ds(pl.multiple_of((origin + o) * 16, 16), 16 * run) for o in offsets]

    def send_stage(c, s):
        if s < p.bits - 1:
            at = 0
            for rows in pieces(c, s, False):
                send[c][s][at : at + rows.size, :] = acc[c][rows, :].astype(BF16)
                at += rows.size
            to = partner[p.orders[c % 2][::-1][s]]
            flights[c] = copy(send[c][s], recv[c][s], to, (rs_send, rs_recv))
        else:
            rows = pl.ds(pl.multiple_of(block + 8 * (1 - bit[top]), 8), 8)
            flights[c] = copy(acc[c].at[rows], last[c], partner[top], (rs_send, rs_recv))
        flights[c].start()
        sent.append(flights[c])

    loads[3].wait()
    loads[4].wait()
    for c, (lo, hi) in enumerate(p.chunks):
        acc[c][...] = scale * jnp.dot(
            hid[...], v_down[:, lo:hi], preferred_element_type=F32
        ) - by_rows(feat[...], v_dec[lo:hi, :])
        send_stage(c, 0)
    for s in range(p.bits - 1):
        for c in range(chunks):
            flights[c].wait_recv()
            at = 0
            for rows in pieces(c, s, True):
                acc[c][rows, :] = acc[c][rows, :] + recv[c][s][at : at + rows.size, :].astype(F32)
                at += rows.size
            send_stage(c, s + 1)
    rows = pl.ds(pl.multiple_of(block + 8 * bit[top], 8), 8)
    for c, (lo, hi) in enumerate(p.chunks):
        flights[c].wait_recv()
        out[:, lo:hi] = acc[c][rows, :] + last[c][...]
    for c in sent:
        c.wait_send()


def shards(tokens, routes, gates, w_gate, w_up, w_down, w_enc, b_enc, w_dec, b_dec):
    n = lax.axis_size("expert")
    d = tokens.shape[1]
    p = Plan(n, d)
    widths = [hi - lo for lo, hi in p.chunks]
    stage_rows = [p.rows // 2 ** (s + 1) for s in range(p.bits - 1)]
    ag = PAIRS + PAIRS * sum(len(p.split(o[:s])[2]) for o in p.orders for s in range(p.bits - 1))
    rs = len(widths) * p.bits
    vmem = pl.BlockSpec(memory_space=pltpu.VMEM)
    hbm = pl.BlockSpec(memory_space=pl.ANY)
    scratch = [
        pltpu.VMEM(w_gate.shape[:0:-1], BF16),
        pltpu.VMEM(w_up.shape[:0:-1], BF16),
        pltpu.VMEM(w_down.shape[1:], BF16),
        pltpu.VMEM(w_enc.shape, BF16),
        pltpu.VMEM(w_dec.shape[::-1], BF16),
        pltpu.VMEM((8, p.wide), F32),
        pltpu.VMEM((PAIRS, 16, p.fold), BF16),
        pltpu.VMEM((PAIRS, 16, p.fold), BF16),
        pltpu.VMEM((p.rows, w_gate.shape[2]), BF16),
        pltpu.VMEM((p.rows, w_enc.shape[1]), BF16),
        pltpu.VMEM((p.rows, w_gate.shape[2]), F32),
        pltpu.VMEM((p.rows, w_gate.shape[2]), F32),
        pltpu.VMEM((p.rows, w_enc.shape[1]), F32),
    ]
    scratch += [pltpu.VMEM((p.rows, hi - lo), BF16) for lo, hi in p.parts]
    scratch += [pltpu.VMEM((p.rows, w), F32) for w in widths]
    scratch += [pltpu.VMEM((r, w), BF16) for w in widths for r in stage_rows] * 2
    scratch += [pltpu.VMEM((8, w), F32) for w in widths]
    scratch += [pltpu.SemaphoreType.DMA((k,)) for k in (5, ag, ag, rs, rs)]
    flops = 2 * p.rows * d * (3 * w_gate.shape[2] + 2 * w_enc.shape[1])
    size = 2 * d * (3 * w_gate.shape[2] + 2 * w_enc.shape[1])
    total = pl.pallas_call(
        functools.partial(body, p),
        out_shape=jax.ShapeDtypeStruct(tokens.shape, F32),
        in_specs=[vmem, vmem, vmem, hbm, hbm, hbm, hbm, vmem, hbm],
        out_specs=vmem,
        scratch_shapes=scratch,
        cost_estimate=pl.CostEstimate(flops=flops, bytes_accessed=size, transcendentals=0),
        compiler_params=pltpu.CompilerParams(
            collective_id=0, has_side_effects=True, vmem_limit_bytes=56 * 2**20
        ),
    )(
        tokens,
        routes.T,
        gates.T,
        w_gate.transpose(0, 2, 1),
        w_up.transpose(0, 2, 1),
        w_down,
        w_enc,
        b_enc.reshape(1, -1),
        w_dec.T,
    )
    return (total - b_dec).astype(BF16)


def solution(mesh):
    in_specs = (
        P(("group", "expert"), None),
        P(("group", "expert"), None),
        P(("group", "expert"), None),
        P("expert", None, None),
        P("expert", None, None),
        P("expert", None, None),
        P(None, "expert"),
        P("expert"),
        P("expert", None),
        P(),
    )
    out_specs = P(("group", "expert"), None)
    return jax.shard_map(shards, mesh=mesh, in_specs=in_specs, out_specs=out_specs, check_vma=False)
```

```python
import functools

import jax
import jax.numpy as jnp
from jax import lax
from jax.experimental import pallas as pl
from jax.experimental.pallas import tpu as pltpu
from jax.sharding import PartitionSpec as P

SLABS = 4
PAIRS = 3
CHUNKS = 6
LANES = 128
F32 = jnp.float32
BF16 = jnp.bfloat16


def cut(width, parts):
    tiles = -(-width // LANES)
    edges = [LANES * (tiles * i // parts) for i in range(parts)] + [width]
    return list(zip(edges[:-1], edges[1:]))


class Plan:
    def __init__(self, n, d):
        self.n, self.d = n, d
        self.bits = n.bit_length() - 1
        self.half = n // 2
        self.rows = 8 * n
        self.wide = -(-(d + n // SLABS) // LANES) * LANES
        self.parts = cut(self.wide, 2 * PAIRS)
        self.fold = max(hi - lo for lo, hi in self.parts)
        self.chunks = cut(d, CHUNKS)
        low = list(range(self.bits - 2, 0, -1))
        near, turn = low[:-3], low[-3:]
        self.orders = [near + turn[i:] + turn[:i] + [0] for i in range(len(turn))]

    def order(self, c):
        return self.orders[c % len(self.orders)]

    def weight(self, j):
        return 2 ** (self.bits - 2 - j)

    def split(self, done):
        run, rest = 1, list(done)
        j = self.bits - 2
        while j in rest:
            rest.remove(j)
            run *= 2
            j -= 1
        offsets = [0]
        for j in rest:
            offsets = offsets + [o + self.weight(j) for o in offsets]
        return run, rest, sorted(offsets)


def body(plan, tokens, routes, gates, w_gate, w_up, w_down, w_enc, b_enc, w_dec, out, *scratch):
    p = plan
    chunks = len(p.chunks)
    (v_gate, v_up, v_down, v_enc, v_dec, flat, fold, fold_in, hid, feat, sum_gate, sum_up, sum_enc) = scratch[:13]
    rest = list(scratch[13:])
    x = [rest.pop(0) for _ in p.parts]
    acc = [rest.pop(0) for _ in range(chunks)]
    send = [[rest.pop(0) for _ in range(p.bits - 1)] for _ in range(chunks)]
    recv = [[rest.pop(0) for _ in range(p.bits - 1)] for _ in range(chunks)]
    last = [rest.pop(0) for _ in range(chunks)]
    load_sem, ag_send, ag_recv, rs_send, rs_recv = rest

    me = lax.axis_index("expert")
    bit = [(me // 2**j) % 2 for j in range(p.bits)]
    partner = [me + (1 - 2 * bit[j]) * 2**j for j in range(p.bits)]
    top = p.bits - 1

    loads = [
        pltpu.make_async_copy(src, dst, load_sem.at[i])
        for i, (src, dst) in enumerate(
            [
                (w_gate.at[0], v_gate),
                (w_up.at[0], v_up),
                (w_enc, v_enc),
                (w_down.at[0], v_down),
                (w_dec, v_dec),
            ]
        )
    ]
    for load in loads:
        load.start()

    barrier = pltpu.get_barrier_semaphore()
    for j in range(p.bits):
        pl.semaphore_signal(
            barrier, inc=1, device_id={"expert": partner[j]}, device_id_type=pl.DeviceIdType.MESH
        )

    start = p.d // LANES * LANES
    lane = lax.broadcasted_iota(jnp.int32, (8, p.wide - start), 1) - (p.d - start)
    dense = jnp.zeros((8, p.wide - start), F32)
    eye = lax.broadcasted_iota(jnp.int32, (8, 8), 0) == lax.broadcasted_iota(jnp.int32, (8, 8), 1)

    def column(row):
        return jnp.sum(jnp.where(eye, row, 0.0), axis=1, keepdims=True)

    chosen = routes[...].astype(F32)
    weights = gates[...].astype(F32)
    for k in range(routes.shape[0]):
        dense = dense + jnp.where(
            lane.astype(F32) == column(chosen[k : k + 1, :]), column(weights[k : k + 1, :]), 0.0
        )
    flat[:, start:] = dense
    flat[:, : p.d] = tokens[...].astype(F32)
    mine = flat[...]

    def part(c):
        lo, hi = p.parts[c]
        return mine[:, lo:hi]

    def padded(value):
        short = p.fold - value.shape[1]
        return jnp.concatenate([value, jnp.zeros((8, short), F32)], axis=1) if short else value

    for q in range(PAIRS):
        both = [padded(part(2 * q)), padded(part(2 * q + 1))]
        fold[q] = jnp.concatenate(both, axis=0).astype(BF16)

    pl.semaphore_wait(barrier, p.bits)

    count = [0]

    def copy(src, dst, to, sems):
        i = count[0]
        count[0] += 1
        return pltpu.make_async_remote_copy(
            src_ref=src,
            dst_ref=dst,
            send_sem=sems[0].at[i],
            recv_sem=sems[1].at[i],
            device_id={"expert": to},
            device_id_type=pl.DeviceIdType.MESH,
        )

    sent = []
    first = [copy(fold.at[q], fold_in.at[q], partner[top], (ag_send, ag_recv)) for q in range(PAIRS)]
    for c in first:
        c.start()
        sent.append(c)

    def base(fixed):
        total = 0
        for j in fixed:
            total = total + bit[j] * p.weight(j)
        return total

    low_bits = list(range(p.bits - 1))
    block = pl.multiple_of(base(low_bits) * 16, 16)
    pending = [[] for _ in p.parts]

    def gather_stage(c, s):
        order = p.order(c)
        done, j = order[:s], order[s]
        run, extra, offsets = p.split(done)
        origin = base([b for b in low_bits if b not in done])
        pending[c] = []
        for o in offsets:
            rows = pl.ds(pl.multiple_of((origin + o) * 16, 16), 16 * run)
            flight = copy(x[c].at[rows], x[c].at[rows], partner[j], (ag_send, ag_recv))
            flight.start()
            sent.append(flight)
            pending[c].append(flight)

    def arrived(c):
        for flight in pending[c]:
            flight.wait_recv()

    for q in range(PAIRS):
        first[q].wait_recv()
        for half in (0, 1):
            c = 2 * q + half
            a = part(c)
            b = fold_in[q].astype(F32)[8 * half : 8 * half + 8, : a.shape[1]]
            low = jnp.where(bit[top] == 0, a, b)
            high = jnp.where(bit[top] == 0, b, a)
            x[c][pl.ds(block, 16), :] = jnp.concatenate([low, high], axis=0).astype(BF16)
            gather_stage(c, 0)
    for s in range(1, p.bits - 1):
        for c in range(len(p.parts)):
            arrived(c)
            gather_stage(c, s)

    def by_rows(a, b):
        return lax.dot_general(a, b, (((1,), (1,)), ((), ())), preferred_element_type=F32)

    for load in loads[:3]:
        load.wait()
    for c, (lo, hi) in enumerate(p.parts):
        arrived(c)
        hi = min(hi, p.d)
        rows = x[c][:, : hi - lo]
        terms = [
            (sum_gate, by_rows(rows, v_gate[:, lo:hi])),
            (sum_up, by_rows(rows, v_up[:, lo:hi])),
            (sum_enc, jnp.dot(rows, v_enc[lo:hi, :], preferred_element_type=F32)),
        ]
        for total, term in terms:
            total[...] = term if c == 0 else total[...] + term
    gate_pre = sum_gate[...]
    hid[...] = ((sum_up[...] + 1.0) * gate_pre * jax.nn.sigmoid(1.702 * gate_pre)).astype(BF16)
    feat[...] = jnp.maximum(sum_enc[...] + b_enc[...], 0.0).astype(BF16)

    tail = x[-1][:, start - p.parts[-1][0] :].astype(F32)
    lane = lax.broadcasted_iota(jnp.int32, tail.shape, 1) - (p.d - start)
    scale = jnp.sum(jnp.where(lane == me // SLABS, tail, 0.0), axis=1, keepdims=True)

    count[0] = 0
    flights = [None] * chunks

    def pieces(c, s, own):
        order = p.order(c)[::-1]
        j = order[s]
        fixed = order[: s + 1]
        run, extra, offsets = p.split([b for b in low_bits if b not in fixed])
        origin = base(order[:s]) + (bit[j] if own else 1 - bit[j]) * p.weight(j)
        return [pl.ds(pl.multiple_of((origin + o) * 16, 16), 16 * run) for o in offsets]

    def send_stage(c, s):
        if s < p.bits - 1:
            at = 0
            for rows in pieces(c, s, False):
                send[c][s][at : at + rows.size, :] = acc[c][rows, :].astype(BF16)
                at += rows.size
            to = partner[p.order(c)[::-1][s]]
            flights[c] = copy(send[c][s], recv[c][s], to, (rs_send, rs_recv))
        else:
            rows = pl.ds(pl.multiple_of(block + 8 * (1 - bit[top]), 8), 8)
            flights[c] = copy(acc[c].at[rows], last[c], partner[top], (rs_send, rs_recv))
        flights[c].start()
        sent.append(flights[c])

    loads[3].wait()
    loads[4].wait()
    for c, (lo, hi) in enumerate(p.chunks):
        acc[c][...] = scale * jnp.dot(
            hid[...], v_down[:, lo:hi], preferred_element_type=F32
        ) - by_rows(feat[...], v_dec[lo:hi, :])
        send_stage(c, 0)
    for s in range(p.bits - 1):
        for c in range(chunks):
            flights[c].wait_recv()
            at = 0
            for rows in pieces(c, s, True):
                acc[c][rows, :] = acc[c][rows, :] + recv[c][s][at : at + rows.size, :].astype(F32)
                at += rows.size
            send_stage(c, s + 1)
    rows = pl.ds(pl.multiple_of(block + 8 * bit[top], 8), 8)
    for c, (lo, hi) in enumerate(p.chunks):
        flights[c].wait_recv()
        out[:, lo:hi] = acc[c][rows, :] + last[c][...]
    for c in sent:
        c.wait_send()


def shards(tokens, routes, gates, w_gate, w_up, w_down, w_enc, b_enc, w_dec, b_dec):
    n = lax.axis_size("expert")
    d = tokens.shape[1]
    p = Plan(n, d)
    widths = [hi - lo for lo, hi in p.chunks]
    stage_rows = [p.rows // 2 ** (s + 1) for s in range(p.bits - 1)]
    ag = PAIRS + sum(
        len(p.split(p.order(c)[:s])[2]) for c in range(2 * PAIRS) for s in range(p.bits - 1)
    )
    rs = len(widths) * p.bits
    vmem = pl.BlockSpec(memory_space=pltpu.VMEM)
    hbm = pl.BlockSpec(memory_space=pl.ANY)
    scratch = [
        pltpu.VMEM(w_gate.shape[:0:-1], BF16),
        pltpu.VMEM(w_up.shape[:0:-1], BF16),
        pltpu.VMEM(w_down.shape[1:], BF16),
        pltpu.VMEM(w_enc.shape, BF16),
        pltpu.VMEM(w_dec.shape[::-1], BF16),
        pltpu.VMEM((8, p.wide), F32),
        pltpu.VMEM((PAIRS, 16, p.fold), BF16),
        pltpu.VMEM((PAIRS, 16, p.fold), BF16),
        pltpu.VMEM((p.rows, w_gate.shape[2]), BF16),
        pltpu.VMEM((p.rows, w_enc.shape[1]), BF16),
        pltpu.VMEM((p.rows, w_gate.shape[2]), F32),
        pltpu.VMEM((p.rows, w_gate.shape[2]), F32),
        pltpu.VMEM((p.rows, w_enc.shape[1]), F32),
    ]
    scratch += [pltpu.VMEM((p.rows, hi - lo), BF16) for lo, hi in p.parts]
    scratch += [pltpu.VMEM((p.rows, w), F32) for w in widths]
    scratch += [pltpu.VMEM((r, w), BF16) for w in widths for r in stage_rows] * 2
    scratch += [pltpu.VMEM((8, w), F32) for w in widths]
    scratch += [pltpu.SemaphoreType.DMA((k,)) for k in (5, ag, ag, rs, rs)]
    flops = 2 * p.rows * d * (3 * w_gate.shape[2] + 2 * w_enc.shape[1])
    size = 2 * d * (3 * w_gate.shape[2] + 2 * w_enc.shape[1])
    total = pl.pallas_call(
        functools.partial(body, p),
        out_shape=jax.ShapeDtypeStruct(tokens.shape, F32),
        in_specs=[vmem, vmem, vmem, hbm, hbm, hbm, hbm, vmem, hbm],
        out_specs=vmem,
        scratch_shapes=scratch,
        cost_estimate=pl.CostEstimate(flops=flops, bytes_accessed=size, transcendentals=0),
        compiler_params=pltpu.CompilerParams(
            collective_id=0, has_side_effects=True, vmem_limit_bytes=56 * 2**20
        ),
    )(
        tokens,
        routes.T,
        gates.T,
        w_gate.transpose(0, 2, 1),
        w_up.transpose(0, 2, 1),
        w_down,
        w_enc,
        b_enc.reshape(1, -1),
        w_dec.T,
    )
    return (total - b_dec).astype(BF16)


def solution(mesh):
    in_specs = (
        P(("group", "expert"), None),
        P(("group", "expert"), None),
        P(("group", "expert"), None),
        P("expert", None, None),
        P("expert", None, None),
        P("expert", None, None),
        P(None, "expert"),
        P("expert"),
        P("expert", None),
        P(),
    )
    out_specs = P(("group", "expert"), None)
    return jax.shard_map(shards, mesh=mesh, in_specs=in_specs, out_specs=out_specs, check_vma=False)
```
